32 devices in a mesh: grp: 4 (over x, core), seq: 8 (over z, y).
Axes of the slice: x: 2, y: 2, z: 4, core: 2. Of those that a mesh axis runs over, the one named last changes fastest.
Arguments:
- queries: bfloat16 [16384, 1024], P(('grp', 'seq')), may hold values from -8 to 8
- keys: bfloat16 [16384, 1024], P(('grp', 'seq')), may hold values from -8 to 8
- values: bfloat16 [16384, 1024], P(('grp', 'seq')), may hold values from -6 to 6
- event_ids: int32 [16384], P(('grp', 'seq')), may hold values from 0 to 511
- type_bias: float32 [512, 16], replicated, may hold values from -4 to 4
- block_start: int32 [32, 5], P(('grp', 'seq')), may hold values from 0 to 448
- d_out: bfloat16 [16384, 1024], P(('grp', 'seq')), may hold values from -6 to 6
Outputs:
- out: bfloat16 [16384, 1024], P(('grp', 'seq'))
- d_queries: bfloat16 [16384, 1024], P(('grp', 'seq'))
- d_keys: bfloat16 [16384, 1024], P(('grp', 'seq'))
- d_values: bfloat16 [16384, 1024], P(('grp', 'seq'))
The draws below stay inside these ranges and needn't reach their ends.
All inputs are finite; a program needn't handle non-finite values.
Results may differ from the reference program's by a relative error of at most 0.011.
Values may be sent and summed in bfloat16 or wider, within the bound.
A program may use at most 128 MiB of HBM per device.

```python
import math
import jax
import jax.numpy as jnp
import numpy as np
from jax import lax

H = 16
DH = 64
D = 1024
TYPES = 512
WIN = 256
BLK = 64
TOK_DEV = 512
LEVELS = 5
LENGTH = 16384
N_GRP = 4
N_SEQ = 8


def drawn_pair(key):
    width_all = H * DH
    query_seed = jax.random.fold_in(key, 1001)
    key_seed = jax.random.fold_in(key, 1002)
    query_base = jnp.clip(jax.random.normal(query_seed, (LENGTH, width_all), jnp.float32), -6.0, 6.0)
    key_base = jnp.clip(jax.random.normal(key_seed, (LENGTH, width_all), jnp.float32), -6.0, 6.0)
    return (query_base, key_base)


def draw_queries(key, part):
    return drawn_pair(key)[0].astype(jnp.bfloat16)


def draw_keys(key, part):
    return drawn_pair(key)[1].astype(jnp.bfloat16)


def plant(values, key, least, top_value):
    spot = [jax.random.randint(jax.random.fold_in(key, axis), (), 0, length) for axis, length in enumerate(values.shape)]
    longest = values.shape.index(max(values.shape))
    neighbour = spot[:longest] + [(spot[longest] + 1) % values.shape[longest]] + spot[longest + 1:]
    return values.at[tuple(spot)].set(least).at[tuple(neighbour)].set(top_value)


def block_scale(stream_key, extent, split, smallest, top_value):
    loudness, own = 1.0, jax.random.fold_in(stream_key, 6)
    for axis_at, parts in split:
        heights = jnp.exp(jax.random.uniform(jax.random.fold_in(own, axis_at), (parts,), jnp.float32, smallest / len(split), top_value / len(split)))
        loudness = loudness * jnp.repeat(heights, extent[axis_at] // parts).reshape([-1 if axis == axis_at else 1 for axis in range(len(extent))])
    return loudness


def cumulative_ranks(amount, slope):
    weights = [(1 << 20) // math.isqrt(grade ** slope) + 1 for grade in range(1, amount + 1)]
    spread = 1 + sum(weights) // (1 << 30)
    return np.cumsum(np.array([max(1, weight // spread) for weight in weights]))


def skewed_ids(stream_key, dims, count, lean):
    grid = cumulative_ranks(count, lean)
    lot = jax.random.randint(jax.random.fold_in(stream_key, 1), dims, 0, int(grid[count - 1]))
    standing = jnp.searchsorted(jnp.asarray(grid, jnp.int32), lot, side="right")
    return jax.random.permutation(jax.random.fold_in(stream_key, 2), count)[standing].astype(jnp.int32)


def noise(key, extent, deviation, bound, pieces=(), held_as=jnp.bfloat16):
    gain = block_scale(key, extent, pieces, -0.22, 0.18) if pieces else 1.0
    values = jax.random.normal(key, extent, jnp.float32) * deviation * gain
    return jnp.minimum(jnp.maximum(values, -bound), bound).astype(held_as)


def setup_inputs(seed: int = 0) -> dict:
    key_of = jax.random.split(jax.random.key(seed), 8)
    return {
        "queries": draw_queries(jax.random.fold_in(key_of[7], 71), 0),
        "keys": draw_keys(jax.random.fold_in(key_of[7], 71), 0),
        "values": noise(key_of[2], (LENGTH, D), 1.0, 6.0, ((0, 32),)),
        "event_ids": plant(skewed_ids(key_of[3], (LENGTH,), TYPES, 2), jax.random.fold_in(key_of[3], 3), 0, TYPES - 1).astype(jnp.int32),
        "type_bias": noise(key_of[4], (TYPES, H), 1.0, 4.0, (), jnp.float32),
        "block_start": plant(jax.random.randint(key_of[5], (N_GRP * N_SEQ, LEVELS), 0, TOK_DEV - BLK + 1), jax.random.fold_in(key_of[5], 1), 0, TOK_DEV - BLK).astype(jnp.int32),
        "d_out": noise(key_of[6], (LENGTH, D), 1.0, 6.0, ((0, 32),)),
    }


def device_pass(inputs):
    query_rows, grad_rows, near_keys, near_values, near_bias, far_keys, far_values, far_bias, tail_live, far_live = inputs
    exact_mode = lax.Precision.HIGHEST
    score_scale = 1.0 / math.sqrt(DH)

    def split_heads(array):
        return array.astype(jnp.float32).reshape(array.shape[0], H, DH)
    query_heads = split_heads(query_rows)
    grad_heads = split_heads(grad_rows)
    near_key_heads = split_heads(near_keys)
    near_value_heads = split_heads(near_values)
    far_key_heads = split_heads(far_keys)
    far_value_heads = split_heads(far_values)
    row_index = jnp.arange(TOK_DEV)[:, None]
    col_index = jnp.arange(WIN + TOK_DEV)[None, :]
    near_mask = (col_index >= row_index) & (col_index <= row_index + WIN) & ((col_index >= WIN) | tail_live)
    near_scores = jnp.einsum('qhd,khd->hqk', query_heads, near_key_heads, precision=exact_mode) * score_scale
    near_scores = near_scores + near_bias.astype(jnp.float32).T[:, None, :]
    far_scores = jnp.einsum('qhd,khd->hqk', query_heads, far_key_heads, precision=exact_mode) * score_scale
    far_scores = far_scores + far_bias.astype(jnp.float32).T[:, None, :]
    near_scores = jnp.where(near_mask[None], near_scores, -jnp.inf)
    far_scores = jnp.where(far_live[None, None, :], far_scores, -jnp.inf)
    highest = jnp.maximum(lax.optimization_barrier(jnp.max(near_scores, axis=-1)), lax.optimization_barrier(jnp.max(far_scores, axis=-1)))[:, :, None]
    near_exp = jnp.exp(near_scores - highest)
    far_exp = jnp.exp(far_scores - highest)
    normalizer = lax.optimization_barrier(jnp.sum(near_exp, axis=-1, keepdims=True)) + lax.optimization_barrier(jnp.sum(far_exp, axis=-1, keepdims=True))
    near_weights = near_exp / normalizer
    far_weights = far_exp / normalizer
    near_rounded = lax.optimization_barrier(near_weights.astype(jnp.bfloat16)).astype(jnp.float32)
    far_rounded = lax.optimization_barrier(far_weights.astype(jnp.bfloat16)).astype(jnp.float32)
    attended = jnp.einsum('hqk,khd->qhd', near_rounded, near_value_heads, precision=exact_mode)
    attended = attended + jnp.einsum('hqk,khd->qhd', far_rounded, far_value_heads, precision=exact_mode)
    row_dot = lax.optimization_barrier(jnp.sum(grad_heads * attended, axis=-1)).T[:, :, None]
    near_dw = jnp.einsum('qhd,khd->hqk', grad_heads, near_value_heads, precision=exact_mode)
    far_dw = jnp.einsum('qhd,khd->hqk', grad_heads, far_value_heads, precision=exact_mode)
    near_ds = lax.optimization_barrier((near_weights * (near_dw - row_dot)).astype(jnp.bfloat16)).astype(jnp.float32)
    far_ds = lax.optimization_barrier((far_weights * (far_dw - row_dot)).astype(jnp.bfloat16)).astype(jnp.float32)
    query_grad = jnp.einsum('hqk,khd->qhd', near_ds, near_key_heads, precision=exact_mode)
    query_grad = (query_grad + jnp.einsum('hqk,khd->qhd', far_ds, far_key_heads, precision=exact_mode)) * score_scale
    near_key_grad = jnp.einsum('hqk,qhd->khd', near_ds, query_heads, precision=exact_mode) * score_scale
    near_value_grad = jnp.einsum('hqk,qhd->khd', near_rounded, grad_heads, precision=exact_mode)
    far_key_grad = jnp.einsum('hqk,qhd->khd', far_ds, query_heads, precision=exact_mode) * score_scale
    far_value_grad = jnp.einsum('hqk,qhd->khd', far_rounded, grad_heads, precision=exact_mode)
    width_all = H * DH
    return (attended.reshape(TOK_DEV, width_all).astype(jnp.bfloat16), query_grad.reshape(TOK_DEV, width_all).astype(jnp.bfloat16), near_key_grad.reshape(WIN + TOK_DEV, width_all), near_value_grad.reshape(WIN + TOK_DEV, width_all), far_key_grad.reshape(LEVELS * BLK, width_all), far_value_grad.reshape(LEVELS * BLK, width_all))

def reference(queries, keys, values, event_ids, type_bias, block_start, d_out):
    device_count = N_GRP * N_SEQ
    width_all = H * DH
    key_bias = type_bias[event_ids].astype(jnp.bfloat16)

    def per_device(array):
        return array.reshape(device_count, TOK_DEV, array.shape[-1])
    query_dev = per_device(queries)
    key_dev = per_device(keys)
    value_dev = per_device(values)
    bias_dev = per_device(key_bias)
    grad_dev = per_device(d_out)

    def with_tail(array):
        empty = jnp.zeros_like(array[:1, TOK_DEV - WIN:])
        tails = jnp.concatenate([empty, array[:-1, TOK_DEV - WIN:]], axis=0)
        return jnp.concatenate([tails, array], axis=1)

    def far_blocks(array):

        def pick(rows_of, starts):
            return jnp.stack([lax.dynamic_slice_in_dim(rows_of, starts[degree].astype(jnp.int32), BLK, 0) for degree in range(LEVELS)])
        source = jax.vmap(pick)(array, block_start)
        moved = []
        for degree in range(LEVELS):
            distance = 2 ** degree
            empty = jnp.zeros_like(source[:distance, degree])
            moved.append(jnp.concatenate([empty, source[:device_count - distance, degree]], axis=0))
        return jnp.stack(moved, axis=1).reshape(device_count, LEVELS * BLK, array.shape[-1])
    positions = jnp.arange(device_count, dtype=jnp.int32)
    tail_live = positions >= 1
    level_flags = positions[:, None] >= (2 ** jnp.arange(LEVELS, dtype=jnp.int32))[None, :]
    far_live = jnp.repeat(level_flags, BLK, axis=1)
    results = lax.map(device_pass, (query_dev, grad_dev, with_tail(key_dev), with_tail(value_dev), with_tail(bias_dev), far_blocks(key_dev), far_blocks(value_dev), far_blocks(bias_dev), tail_live, far_live))
    attended_out, query_grad, near_key, near_value, far_key, far_value = results

    def place_block(rows_of, block_rows, start):
        start = start.astype(jnp.int32)
        current = lax.dynamic_slice_in_dim(rows_of, start, BLK, 0)
        return lax.dynamic_update_slice_in_dim(rows_of, current + block_rows, start, 0)

    def settle(near_terms, far_terms):
        own = near_terms[:, WIN:]
        tail_part = lax.optimization_barrier(near_terms[:, :WIN].astype(jnp.bfloat16)).astype(jnp.float32)
        arriving = jnp.concatenate([tail_part[1:], jnp.zeros_like(tail_part[:1])], axis=0)
        own = own.at[:, TOK_DEV - WIN:].add(arriving)
        far_part = lax.optimization_barrier(far_terms.astype(jnp.bfloat16)).astype(jnp.float32)
        far_part = far_part.reshape(device_count, LEVELS, BLK, width_all)
        for degree in range(LEVELS):
            distance = 2 ** degree
            arriving = jnp.concatenate([far_part[distance:, degree], jnp.zeros_like(far_part[:distance, degree])], axis=0)
            own = jax.vmap(place_block)(own, arriving, block_start[:, degree])
        return own.reshape(device_count * TOK_DEV, width_all).astype(jnp.bfloat16)
    return (attended_out.reshape(device_count * TOK_DEV, width_all), query_grad.reshape(device_count * TOK_DEV, width_all), settle(near_key, far_key), settle(near_value, far_value))
```

```python
import functools

import jax
import jax.numpy as jnp
from jax import lax
from jax.experimental import pallas as pl
from jax.experimental.pallas import tpu as pltpu
from jax.sharding import PartitionSpec as P

WIN = 256
BLK = 64
ROWS = 128
LANES = 128
DEAD = -1e30
CHUNKS = 2
AXES = ("grp", "seq")
F32 = jnp.float32
BF16 = jnp.bfloat16


def passed_along(value, axis, steps):
    count = lax.axis_size(axis)
    initial, last = (max(0, -steps), min(count, count - steps))
    return lax.ppermute(value, axis, [(source, source + steps) for source in range(initial, last)])


def nt(a, b):
    return lax.dot_general(a, b, (((1,), (1,)), ((), ())), preferred_element_type=F32)


def nn(a, b):
    return lax.dot_general(a, b, (((1,), (0,)), ((), ())), preferred_element_type=F32)


def block_rows_of(start, rows):
    t = lax.broadcasted_iota(jnp.int32, (BLK, rows), 0)
    j = lax.broadcasted_iota(jnp.int32, (BLK, rows), 1)
    return (j - t == start).astype(F32).astype(BF16)


def prep_kernel(levels, width, starts, ids, table, k, v, *refs):
    bias, padded = refs[0], refs[-1]
    payloads = refs[1:-1]
    rows = k.shape[0]
    types, heads = table.shape
    padded[...] = jnp.zeros_like(padded)
    padded[:, :heads] = table[...].astype(BF16).astype(F32)
    kind = lax.broadcasted_iota(jnp.int32, (types, rows), 0)
    onehot = (kind == ids[...]).astype(F32).astype(BF16)
    bias[...] = lax.dot_general(
        onehot, padded[...].astype(BF16), (((0,), (0,)), ((), ())), preferred_element_type=F32
    ).astype(BF16)
    for e in range(levels):
        pick = block_rows_of(starts[0, e], rows)
        bias_block = nn(pick, bias[...]).astype(BF16)
        for c in range(CHUNKS):
            out = payloads[c * levels + e]
            cols = slice(c * width, (c + 1) * width)
            out[0:BLK, 0:width] = nn(pick, k[:, cols]).astype(BF16)
            out[0:BLK, width : 2 * width] = nn(pick, v[:, cols]).astype(BF16)
            out[0:BLK, 2 * width :] = bias_block
            if e == 0:
                out[BLK:, 0:width] = k[rows - WIN :, cols]
                out[BLK:, width : 2 * width] = v[rows - WIN :, cols]
                out[BLK:, 2 * width :] = bias[rows - WIN :, :]


def merged(pair):
    half = LANES // 2
    return jnp.concatenate([pair[:half, :ROWS], pair[half:, ROWS:]], axis=0)


def attend_pair(head, scale, q, do, near_k, near_v, far_k, far_v, near_kt, near_vt, far_kt, far_vt,
                dot, out, dq, near_dk, near_dv, far_dk, far_dv):
    rows = q.shape[0]
    half = LANES // 2
    lane = lax.broadcasted_iota(jnp.int32, (ROWS, LANES), 1)
    first = lane < half
    ones = jnp.concatenate([(lane == head).astype(F32), (lane == head + 1).astype(F32)], axis=0)
    ones = ones.astype(BF16)
    span_row = lax.broadcasted_iota(jnp.int32, (ROWS, 2 * ROWS), 0)
    query_col = lax.broadcasted_iota(jnp.int32, (ROWS, 2 * ROWS), 1) & (ROWS - 1)
    below, above = span_row >= query_col, span_row <= query_col
    span = WIN + ROWS
    zero = jnp.zeros((ROWS, LANES), BF16)
    near_dk[...] = jnp.zeros_like(near_dk)
    near_dv[...] = jnp.zeros_like(near_dv)
    for b in range(rows // ROWS):
        mine = slice(b * ROWS, (b + 1) * ROWS)
        seen = slice(b * ROWS, b * ROWS + span)
        qb = (q[mine, :].astype(F32) * scale).astype(BF16)
        db = do[mine, :]
        q2 = jnp.concatenate([jnp.where(first, qb, zero), jnp.where(first, zero, qb)], axis=0)
        d2 = jnp.concatenate([jnp.where(first, db, zero), jnp.where(first, zero, db)], axis=0)
        qc = jnp.concatenate([q2, ones], axis=1)
        sn = nt(near_k[seen, :], qc)
        sf = nt(far_k[...], qc)
        sn = jnp.concatenate(
            [
                jnp.where(below, sn[:ROWS], DEAD),
                sn[ROWS:WIN],
                jnp.where(above, sn[WIN:], DEAD),
            ],
            axis=0,
        )
        top = jnp.maximum(jnp.max(sn, axis=0, keepdims=True), jnp.max(sf, axis=0, keepdims=True))
        en = jnp.exp(sn - top)
        ef = jnp.exp(sf - top)
        total = jnp.sum(en, axis=0, keepdims=True) + jnp.sum(ef, axis=0, keepdims=True)
        share = 1.0 / total
        wn, wf = en * share, ef * share
        rn, rf = wn.astype(BF16), wf.astype(BF16)
        att = merged(nn(near_vt[:, seen], rn) + nn(far_vt[...], rf))
        out[mine, :] = att.T.astype(out.dtype)
        parts = att * dot[:, mine]
        row_dot = jnp.concatenate(
            [
                jnp.sum(parts[:half], axis=0, keepdims=True),
                jnp.sum(parts[half:], axis=0, keepdims=True),
            ],
            axis=1,
        )
        gn = (wn * (nt(near_v[seen, :], d2) - row_dot)).astype(BF16)
        gf = (wf * (nt(far_v[...], d2) - row_dot)).astype(BF16)
        dqt = merged(nn(near_kt[:, seen], gn) + nn(far_kt[...], gf)) * scale
        dq[mine, :] = dqt.T.astype(dq.dtype)
        near_dk[seen, :] += nn(gn, q2)
        near_dv[seen, :] += nn(rn, d2)
        if b == 0:
            far_dk[...] = nn(gf, q2)
            far_dv[...] = nn(rf, d2)
        else:
            far_dk[...] += nn(gf, q2)
            far_dv[...] += nn(rf, d2)


def load_pair(levels, position, column, k, v, bias, payload_of, near_k, near_v, far_k, far_v,
              near_kt, near_vt, far_kt, far_vt, dot, do):
    near_k[WIN:, :LANES] = k[...]
    near_k[WIN:, LANES:] = bias[...]
    near_v[WIN:, :] = v[...]
    for e in range(levels):
        keys, values, biases = payload_of(e)
        biases = jnp.where(position >= 2**e, biases, jnp.full_like(biases, DEAD))
        at = slice(e * BLK, (e + 1) * BLK)
        far_k[at, :LANES] = keys[:BLK]
        far_k[at, LANES:] = biases[:BLK]
        far_v[at, :] = values[:BLK]
        if e == 0:
            near_k[:WIN, :LANES] = keys[BLK:]
            near_k[:WIN, LANES:] = biases[BLK:]
            near_v[:WIN, :] = values[BLK:]
    near_kt[...] = near_k[:, :LANES].T
    near_vt[...] = near_v[...].T
    far_kt[...] = far_k[:, :LANES].T
    far_vt[...] = far_v[...].T
    dot[...] = do[...].astype(F32).T


def attend_kernel(levels, base, scale, place, q, k, v, do, bias, *refs):
    payloads = refs[: 3 * levels]
    out, dq, own_dk, own_dv = refs[3 * levels : 3 * levels + 4]
    back = refs[3 * levels + 4 : 3 * levels + 4 + 2 * levels]
    (near_k, near_v, far_k, far_v, near_kt, near_vt, far_kt, far_vt, dot, near_dk, near_dv,
     far_dk, far_dv) = refs[3 * levels + 4 + 2 * levels :]
    position = place[0]
    load_pair(
        levels, position, 0, k, v, bias,
        lambda e: tuple(payloads[3 * e + i][...] for i in range(3)),
        near_k, near_v, far_k, far_v, near_kt, near_vt, far_kt, far_vt, dot, do,
    )
    head = 2 * (base + pl.program_id(0))
    attend_pair(head, scale, q, do, near_k, near_v, far_k, far_v, near_kt, near_vt, far_kt,
                far_vt, dot, out, dq, near_dk, near_dv, far_dk, far_dv)
    own_dk[...] = near_dk[WIN:, :]
    own_dv[...] = near_dv[WIN:, :]
    for e in range(levels):
        at = slice(e * BLK, (e + 1) * BLK)
        for ref, far, near in ((back[2 * e], far_dk, near_dk), (back[2 * e + 1], far_dv, near_dv)):
            ref[:BLK, :] = far[at, :].astype(BF16)
            if e == 0:
                ref[BLK:, :] = near[:WIN, :].astype(BF16)


def settle_kernel(levels, starts, own_dk, own_dv, *refs):
    back = refs[: 2 * levels]
    dk, dv = refs[2 * levels :]
    rows = own_dk.shape[0]
    for which, own, final in ((0, own_dk, dk), (1, own_dv, dv)):
        total = own[...]
        for e in range(levels):
            place = block_rows_of(starts[0, e], rows)
            arrived = back[2 * e + which]
            total = total + lax.dot_general(
                place, arrived[:BLK, :], (((0,), (0,)), ((), ())), preferred_element_type=F32
            )
        first = rows - WIN
        final[:first, :] = total[:first].astype(BF16)
        final[first:, :] = (total[first:] + back[which][BLK:, :].astype(F32)).astype(BF16)


def local(queries, keys, values, event_ids, type_bias, block_start, d_out):
    rows, width_all = queries.shape
    heads = type_bias.shape[1]
    levels = block_start.shape[1]
    scale = (width_all // heads) ** -0.5
    width = width_all // CHUNKS
    pairs = width // LANES
    far = levels * BLK
    sds = jax.ShapeDtypeStruct
    smem = pl.BlockSpec(memory_space=pltpu.SMEM)
    vmem = pl.BlockSpec(memory_space=pltpu.VMEM)
    depth = [BLK + (WIN if e == 0 else 0) for e in range(levels)]
    params = pltpu.CompilerParams(vmem_limit_bytes=48 * 2**20)

    prepared = pl.pallas_call(
        functools.partial(prep_kernel, levels, width),
        out_shape=[sds((rows, LANES), BF16)]
        + [sds((depth[e], 2 * width + LANES), BF16) for _ in range(CHUNKS) for e in range(levels)],
        in_specs=[smem, vmem, vmem, vmem, vmem],
        out_specs=[vmem] * (1 + CHUNKS * levels),
        scratch_shapes=[pltpu.VMEM((type_bias.shape[0], LANES), F32)],
        compiler_params=params,
        name="prep",
    )(block_start, event_ids[None, :], type_bias, keys, values)
    bias, payloads = prepared[0], prepared[1:]
    position = lax.axis_index(AXES).astype(jnp.int32)[None]

    arrived = [
        [passed_along(payloads[c * levels + e], AXES, 2**e) for e in range(levels)]
        for c in range(CHUNKS)
    ]
    parts = []
    returned = []
    for c in range(CHUNKS):
        base = c * pairs

        def column(p, base=base):
            return (0, base + p)

        def own_column(p):
            return (0, p)

        wide = pl.BlockSpec((rows, LANES), column)
        narrow = pl.BlockSpec((rows, LANES), own_column)
        specs, operands = [], []
        for e in range(levels):
            for i in range(3):
                specs.append(
                    pl.BlockSpec(
                        (depth[e], LANES),
                        (lambda p, i=i: (0, i * pairs + p)) if i < 2 else (lambda p: (0, 2 * pairs)),
                    )
                )
                operands.append(arrived[c][e])
        cost = 12 * rows * (WIN + ROWS + far) * width
        res = pl.pallas_call(
            functools.partial(attend_kernel, levels, base, scale),
            grid=(pairs,),
            out_shape=[sds((rows, width), BF16)] * 2
            + [sds((rows, width), F32)] * 2
            + [sds((depth[e], width), BF16) for e in range(levels) for _ in range(2)],
            in_specs=[smem, wide, wide, wide, wide, pl.BlockSpec((rows, LANES), lambda p: (0, 0))]
            + specs,
            out_specs=[narrow] * 4
            + [pl.BlockSpec((depth[e], LANES), own_column) for e in range(levels) for _ in range(2)],
            scratch_shapes=[
                pltpu.VMEM((WIN + rows, 2 * LANES), BF16),
                pltpu.VMEM((WIN + rows, LANES), BF16),
                pltpu.VMEM((far, 2 * LANES), BF16),
                pltpu.VMEM((far, LANES), BF16),
                pltpu.VMEM((LANES, WIN + rows), BF16),
                pltpu.VMEM((LANES, WIN + rows), BF16),
                pltpu.VMEM((LANES, far), BF16),
                pltpu.VMEM((LANES, far), BF16),
                pltpu.VMEM((LANES, rows), F32),
                pltpu.VMEM((WIN + rows, LANES), F32),
                pltpu.VMEM((WIN + rows, LANES), F32),
                pltpu.VMEM((far, LANES), F32),
                pltpu.VMEM((far, LANES), F32),
            ],
            compiler_params=params,
            cost_estimate=pl.CostEstimate(
                flops=cost * 4, bytes_accessed=16 * rows * width, transcendentals=0
            ),
            name="attend",
        )(position, queries, keys, values, d_out, bias, *operands)
        parts.append(res[:4])
        returned.append(
            [passed_along(tuple(res[4 + 2 * e : 6 + 2 * e]), AXES, -(2**e)) for e in range(levels)]
        )
    finals = []
    for c in range(CHUNKS):
        step = min(width, 256)
        block = pl.BlockSpec((rows, step), lambda p: (0, p))
        finals.append(
            pl.pallas_call(
                functools.partial(settle_kernel, levels),
                grid=(width // step,),
                out_shape=[sds((rows, width), BF16)] * 2,
                in_specs=[smem, block, block]
                + [
                    pl.BlockSpec((depth[e], step), lambda p: (0, p))
                    for e in range(levels)
                    for _ in range(2)
                ],
                out_specs=[block] * 2,
                compiler_params=params,
                name="settle",
            )(block_start, parts[c][2], parts[c][3], *[a for pair in returned[c] for a in pair])
        )
    return tuple(
        jnp.concatenate(list(chunk), axis=1)
        for chunk in (
            [p[0] for p in parts],
            [p[1] for p in parts],
            [f[0] for f in finals],
            [f[1] for f in finals],
        )
    )


def solution(mesh):
    rows = P(AXES, None)
    return jax.shard_map(
        local,
        mesh=mesh,
        in_specs=(rows, rows, rows, P(AXES), P(), rows, rows),
        out_specs=(rows, rows, rows, rows),
        check_vma=False,
    )
```

```python
import functools

import jax
import jax.numpy as jnp
from jax import lax
from jax.experimental import pallas as pl
from jax.experimental.pallas import tpu as pltpu
from jax.sharding import PartitionSpec as P

WIN = 256
BLK = 64
ROWS = 128
LANES = 128
DEAD = -1e30
AHEAD = 3
AXES = ("grp", "seq")
F32 = jnp.float32
BF16 = jnp.bfloat16


def nt(a, b):
    return lax.dot_general(a, b, (((1,), (1,)), ((), ())), preferred_element_type=F32)


def nn(a, b):
    return lax.dot_general(a, b, (((1,), (0,)), ((), ())), preferred_element_type=F32)


def block_rows_of(start, rows):
    t = lax.broadcasted_iota(jnp.int32, (BLK, rows), 0)
    j = lax.broadcasted_iota(jnp.int32, (BLK, rows), 1)
    return (j - t == start).astype(F32).astype(BF16)


def merged(pair):
    half = LANES // 2
    return jnp.concatenate([pair[:half, :ROWS], pair[half:, ROWS:]], axis=0)


def attend_pair(head, scale, q, do, near_k, near_v, far_k, far_v, near_kt, near_vt, far_kt, far_vt,
                dot, out, dq, near_dk, near_dv, far_dk, far_dv):
    rows = q.shape[0]
    half = LANES // 2
    lane = lax.broadcasted_iota(jnp.int32, (ROWS, LANES), 1)
    first = lane < half
    ones = jnp.concatenate([(lane == head).astype(F32), (lane == head + 1).astype(F32)], axis=0)
    ones = ones.astype(BF16)
    span_row = lax.broadcasted_iota(jnp.int32, (ROWS, 2 * ROWS), 0)
    query_col = lax.broadcasted_iota(jnp.int32, (ROWS, 2 * ROWS), 1) & (ROWS - 1)
    below, above = span_row >= query_col, span_row <= query_col
    span = WIN + ROWS
    zero = jnp.zeros((ROWS, LANES), BF16)
    near_dk[...] = jnp.zeros_like(near_dk)
    near_dv[...] = jnp.zeros_like(near_dv)
    for b in range(rows // ROWS):
        mine = slice(b * ROWS, (b + 1) * ROWS)
        seen = slice(b * ROWS, b * ROWS + span)
        qb = (q[mine, :].astype(F32) * scale).astype(BF16)
        db = do[mine, :]
        q2 = jnp.concatenate([jnp.where(first, qb, zero), jnp.where(first, zero, qb)], axis=0)
        d2 = jnp.concatenate([jnp.where(first, db, zero), jnp.where(first, zero, db)], axis=0)
        qc = jnp.concatenate([q2, ones], axis=1)
        sn = nt(near_k[seen, :], qc)
        sf = nt(far_k[...], qc)
        sn = jnp.concatenate(
            [
                jnp.where(below, sn[:ROWS], DEAD),
                sn[ROWS:WIN],
                jnp.where(above, sn[WIN:], DEAD),
            ],
            axis=0,
        )
        top = jnp.maximum(jnp.max(sn, axis=0, keepdims=True), jnp.max(sf, axis=0, keepdims=True))
        en = jnp.exp(sn - top)
        ef = jnp.exp(sf - top)
        total = jnp.sum(en, axis=0, keepdims=True) + jnp.sum(ef, axis=0, keepdims=True)
        share = 1.0 / total
        wn, wf = en * share, ef * share
        rn, rf = wn.astype(BF16), wf.astype(BF16)
        att = merged(nn(near_vt[:, seen], rn) + nn(far_vt[...], rf))
        out[mine, :] = att.T.astype(out.dtype)
        parts = att * dot[:, mine]
        row_dot = jnp.concatenate(
            [
                jnp.sum(parts[:half], axis=0, keepdims=True),
                jnp.sum(parts[half:], axis=0, keepdims=True),
            ],
            axis=1,
        )
        gn = (wn * (nt(near_v[seen, :], d2) - row_dot)).astype(BF16)
        gf = (wf * (nt(far_v[...], d2) - row_dot)).astype(BF16)
        dqt = merged(nn(near_kt[:, seen], gn) + nn(far_kt[...], gf)) * scale
        dq[mine, :] = dqt.T.astype(dq.dtype)
        near_dk[seen, :] += nn(gn, q2)
        near_dv[seen, :] += nn(rn, d2)
        if b == 0:
            far_dk[...] = nn(gf, q2)
            far_dv[...] = nn(rf, d2)
        else:
            far_dk[...] += nn(gf, q2)
            far_dv[...] += nn(rf, d2)


def tn(a, b):
    return lax.dot_general(a, b, (((0,), (0,)), ((), ())), preferred_element_type=F32)


def kernel(levels, scale, starts, ids, table, q, k, v, do, out, dq, dk, dv, bias, padded,
           send_f, recv_f, send_bias, recv_bias, send_b, recv_b, own,
           near_k, near_v, far_k, far_v, near_kt, near_vt, far_kt, far_vt, dot,
           near_dk, near_dv, far_dk, far_dv,
           sem_fs, sem_fr, sem_bias_s, sem_bias_r, sem_bs, sem_br):
    rows, width_all = q.shape
    pairs = width_all // LANES
    ahead = min(AHEAD, pairs)
    types, heads = table.shape
    lines = lax.axis_size("seq")
    count = lax.axis_size("grp") * lines
    position = lax.axis_index("grp") * lines + lax.axis_index("seq")
    depth = [BLK + (WIN if e == 0 else 0) for e in range(levels)]
    offset = [sum(depth[:e]) for e in range(levels)]
    spot = [pl.ds(offset[e], depth[e]) for e in range(levels)]

    def device(index):
        return (lax.div(index, lines), lax.rem(index, lines))

    def takes(e):
        return position >= 2**e

    def gives(e):
        return position + 2**e < count

    def copy(src, dst, send, recv, index):
        return pltpu.make_async_remote_copy(
            src_ref=src, dst_ref=dst, send_sem=send, recv_sem=recv,
            device_id=device(index), device_id_type=pl.DeviceIdType.MESH,
        )

    def ahead_copy(p, e):
        return copy(send_f.at[p, spot[e]], recv_f.at[p, spot[e]], sem_fs.at[p, e],
                    sem_fr.at[p, e], position + 2**e)

    def bias_copy(e):
        return copy(send_bias.at[spot[e]], recv_bias.at[spot[e]], sem_bias_s.at[e],
                    sem_bias_r.at[e], position + 2**e)

    def back_copy(p, e):
        return copy(send_b.at[p, spot[e]], recv_b.at[p, spot[e]], sem_bs.at[p, e],
                    sem_br.at[p, e], position - 2**e)

    barrier = pltpu.get_barrier_semaphore()
    for e in range(levels):

        @pl.when(gives(e))
        def _():
            pl.semaphore_signal(barrier, inc=1, device_id=device(position + 2**e),
                                device_id_type=pl.DeviceIdType.MESH)

        @pl.when(takes(e))
        def _():
            pl.semaphore_signal(barrier, inc=1, device_id=device(position - 2**e),
                                device_id_type=pl.DeviceIdType.MESH)

    padded[...] = jnp.zeros_like(padded)
    padded[:, :heads] = table[...].astype(BF16).astype(F32)
    kind = lax.broadcasted_iota(jnp.int32, (types, rows), 0)
    onehot = (kind == ids[...]).astype(F32).astype(BF16)
    bias[...] = tn(onehot, padded[...].astype(BF16)).astype(BF16)
    for e in range(levels):
        pick = block_rows_of(starts[0, e], rows)
        send_bias[offset[e] : offset[e] + BLK, :] = nn(pick, bias[...]).astype(BF16)
        if e == 0:
            send_bias[BLK : BLK + WIN, :] = bias[rows - WIN :, :]

        @pl.when(jnp.logical_not(takes(e)))
        def _():
            recv_bias[spot[e], :] = jnp.full((depth[e], LANES), DEAD, BF16)

            def clear(p, carry):
                recv_f[p, spot[e], :] = jnp.zeros((depth[e], 2 * LANES), BF16)
                return carry

            lax.fori_loop(0, pairs, clear, 0)

        @pl.when(jnp.logical_not(gives(e)))
        def _():
            def clear(p, carry):
                recv_b[p, spot[e], :] = jnp.zeros((depth[e], 2 * LANES), BF16)
                return carry

            lax.fori_loop(0, pairs, clear, 0)

    def columns(p):
        return pl.ds(pl.multiple_of(p * LANES, LANES), LANES)

    def gather(p):
        both = jnp.concatenate([k[:, columns(p)], v[:, columns(p)]], axis=1)
        for e in range(levels):
            pick = block_rows_of(starts[0, e], rows)
            send_f[p, offset[e] : offset[e] + BLK, :] = nn(pick, both).astype(BF16)
            if e == 0:
                send_f[p, BLK : BLK + WIN, :] = both[rows - WIN :]

    def send_ahead(p):
        for e in range(levels):

            @pl.when(gives(e))
            def _():
                ahead_copy(p, e).start()

    gather(0)
    greeted = 0
    for e in range(levels):
        greeted = greeted + gives(e).astype(jnp.int32) + takes(e).astype(jnp.int32)
    pl.semaphore_wait(barrier, greeted)
    for e in range(levels):

        @pl.when(gives(e))
        def _():
            bias_copy(e).start()

    send_ahead(0)

    def early(p, carry):
        gather(p)
        send_ahead(p)
        return carry

    lax.fori_loop(1, ahead, early, 0)
    for e in range(levels):

        @pl.when(takes(e))
        def _():
            bias_copy(e).wait_recv()

    near_k[:WIN, LANES:] = recv_bias[BLK : BLK + WIN, :]
    near_k[WIN:, LANES:] = bias[...]
    for e in range(levels):
        far_k[e * BLK : (e + 1) * BLK, LANES:] = recv_bias[offset[e] : offset[e] + BLK, :]

    def one_pair(p, carry):
        @pl.when(p + ahead < pairs)
        def _():
            gather(p + ahead)
            send_ahead(p + ahead)

        mine = columns(p)
        near_k[WIN:, :LANES] = k[:, mine]
        near_v[WIN:, :] = v[:, mine]
        dot[...] = do[:, mine].astype(F32).T
        for e in range(levels):

            @pl.when(takes(e))
            def _():
                ahead_copy(p, e).wait_recv()

        for e in range(levels):
            at = slice(e * BLK, (e + 1) * BLK)
            far_k[at, :LANES] = recv_f[p, offset[e] : offset[e] + BLK, :LANES]
            far_v[at, :] = recv_f[p, offset[e] : offset[e] + BLK, LANES:]
        near_k[:WIN, :LANES] = recv_f[p, BLK : BLK + WIN, :LANES]
        near_v[:WIN, :] = recv_f[p, BLK : BLK + WIN, LANES:]
        near_kt[...] = near_k[:, :LANES].T
        near_vt[...] = near_v[...].T
        far_kt[...] = far_k[:, :LANES].T
        far_vt[...] = far_v[...].T
        attend_pair(2 * p, scale, q.at[:, mine], do.at[:, mine], near_k, near_v, far_k, far_v,
                    near_kt, near_vt, far_kt, far_vt, dot, out.at[:, mine], dq.at[:, mine],
                    near_dk, near_dv, far_dk, far_dv)
        for e in range(levels):
            at = slice(e * BLK, (e + 1) * BLK)
            send_b[p, offset[e] : offset[e] + BLK, :LANES] = far_dk[at, :].astype(BF16)
            send_b[p, offset[e] : offset[e] + BLK, LANES:] = far_dv[at, :].astype(BF16)
            if e == 0:
                send_b[p, BLK : BLK + WIN, :LANES] = near_dk[:WIN, :].astype(BF16)
                send_b[p, BLK : BLK + WIN, LANES:] = near_dv[:WIN, :].astype(BF16)

            @pl.when(takes(e))
            def _():
                back_copy(p, e).start()

        own[p, :, :LANES] = near_dk[WIN:, :]
        own[p, :, LANES:] = near_dv[WIN:, :]
        return carry

    lax.fori_loop(0, pairs, one_pair, 0)

    def settle(p, carry):
        for e in range(levels):

            @pl.when(gives(e))
            def _():
                back_copy(p, e).wait_recv()

        total = own[p]
        for e in range(levels):
            total = total + tn(
                block_rows_of(starts[0, e], rows), recv_b[p, offset[e] : offset[e] + BLK, :]
            )
        first = rows - WIN
        last = total[first:] + recv_b[p, BLK : BLK + WIN, :].astype(F32)
        mine = columns(p)
        dk[:first, mine] = total[:first, :LANES].astype(BF16)
        dv[:first, mine] = total[:first, LANES:].astype(BF16)
        dk[first:, mine] = last[:, :LANES].astype(BF16)
        dv[first:, mine] = last[:, LANES:].astype(BF16)
        return carry

    lax.fori_loop(0, pairs, settle, 0)

    def sent(p, carry):
        for e in range(levels):

            @pl.when(gives(e))
            def _():
                ahead_copy(p, e).wait_send()

            @pl.when(takes(e))
            def _():
                back_copy(p, e).wait_send()

        return carry

    lax.fori_loop(0, pairs, sent, 0)
    for e in range(levels):

        @pl.when(gives(e))
        def _():
            bias_copy(e).wait_send()


def local(queries, keys, values, event_ids, type_bias, block_start, d_out):
    rows, width_all = queries.shape
    types, heads = type_bias.shape
    levels = block_start.shape[1]
    scale = (width_all // heads) ** -0.5
    pairs = width_all // LANES
    far = levels * BLK
    sent = far + WIN
    smem = pl.BlockSpec(memory_space=pltpu.SMEM)
    vmem = pl.BlockSpec(memory_space=pltpu.VMEM)
    dma = pltpu.SemaphoreType.DMA
    return pl.pallas_call(
        functools.partial(kernel, levels, scale),
        out_shape=[jax.ShapeDtypeStruct((rows, width_all), BF16)] * 4,
        in_specs=[smem] + [vmem] * 6,
        out_specs=[vmem] * 4,
        scratch_shapes=[
            pltpu.VMEM((rows, LANES), BF16),
            pltpu.VMEM((types, LANES), F32),
            pltpu.VMEM((pairs, sent, 2 * LANES), BF16),
            pltpu.VMEM((pairs, sent, 2 * LANES), BF16),
            pltpu.VMEM((sent, LANES), BF16),
            pltpu.VMEM((sent, LANES), BF16),
            pltpu.VMEM((pairs, sent, 2 * LANES), BF16),
            pltpu.VMEM((pairs, sent, 2 * LANES), BF16),
            pltpu.VMEM((pairs, rows, 2 * LANES), F32),
            pltpu.VMEM((WIN + rows, 2 * LANES), BF16),
            pltpu.VMEM((WIN + rows, LANES), BF16),
            pltpu.VMEM((far, 2 * LANES), BF16),
            pltpu.VMEM((far, LANES), BF16),
            pltpu.VMEM((LANES, WIN + rows), BF16),
            pltpu.VMEM((LANES, WIN + rows), BF16),
            pltpu.VMEM((LANES, far), BF16),
            pltpu.VMEM((LANES, far), BF16),
            pltpu.VMEM((LANES, rows), F32),
            pltpu.VMEM((WIN + rows, LANES), F32),
            pltpu.VMEM((WIN + rows, LANES), F32),
            pltpu.VMEM((far, LANES), F32),
            pltpu.VMEM((far, LANES), F32),
            dma((pairs, levels)),
            dma((pairs, levels)),
            dma((levels,)),
            dma((levels,)),
            dma((pairs, levels)),
            dma((pairs, levels)),
        ],
        compiler_params=pltpu.CompilerParams(
            vmem_limit_bytes=56 * 2**20, collective_id=0, has_side_effects=True
        ),
        cost_estimate=pl.CostEstimate(
            flops=12 * rows * (WIN + ROWS + far) * width_all,
            bytes_accessed=16 * rows * width_all,
            transcendentals=rows * (WIN + ROWS + far) * heads,
        ),
        name="attend",
    )(block_start, event_ids[None, :], type_bias, queries, keys, values, d_out)


def solution(mesh):
    rows = P(AXES, None)
    return jax.shard_map(
        local,
        mesh=mesh,
        in_specs=(rows, rows, rows, P(AXES), P(), rows, rows),
        out_specs=(rows, rows, rows, rows),
        check_vma=False,
    )
```

```python
import functools

import jax
import jax.numpy as jnp
from jax import lax
from jax.experimental import pallas as pl
from jax.experimental.pallas import tpu as pltpu
from jax.sharding import PartitionSpec as P

WIN = 256
BLK = 64
ROWS = 128
LANES = 128
DEAD = -1e30
AHEAD = 1
AXES = ("grp", "seq")
F32 = jnp.float32
BF16 = jnp.bfloat16


def nt(a, b):
    return lax.dot_general(a, b, (((1,), (1,)), ((), ())), preferred_element_type=F32)


def nn(a, b):
    return lax.dot_general(a, b, (((1,), (0,)), ((), ())), preferred_element_type=F32)


def block_rows_of(start, rows):
    t = lax.broadcasted_iota(jnp.int32, (BLK, rows), 0)
    j = lax.broadcasted_iota(jnp.int32, (BLK, rows), 1)
    return (j - t == start).astype(F32).astype(BF16)


def merged(pair):
    half = LANES // 2
    return jnp.concatenate([pair[:half, :ROWS], pair[half:, ROWS:]], axis=0)


def attend_pair(head, scale, q, do, near_k, near_v, far_k, far_v, near_kt, near_vt, far_kt, far_vt,
                dot, out, dq, near_dk, near_dv, far_dk, far_dv):
    rows = q.shape[0]
    half = LANES // 2
    lane = lax.broadcasted_iota(jnp.int32, (ROWS, LANES), 1)
    first = lane < half
    ones = jnp.concatenate([(lane == head).astype(F32), (lane == head + 1).astype(F32)], axis=0)
    ones = ones.astype(BF16)
    span_row = lax.broadcasted_iota(jnp.int32, (ROWS, 2 * ROWS), 0)
    query_col = lax.broadcasted_iota(jnp.int32, (ROWS, 2 * ROWS), 1) & (ROWS - 1)
    below, above = span_row >= query_col, span_row <= query_col
    span = WIN + ROWS
    zero = jnp.zeros((ROWS, LANES), BF16)
    near_dk[...] = jnp.zeros_like(near_dk)
    near_dv[...] = jnp.zeros_like(near_dv)
    for b in range(rows // ROWS):
        mine = slice(b * ROWS, (b + 1) * ROWS)
        seen = slice(b * ROWS, b * ROWS + span)
        qb = (q[mine, :].astype(F32) * scale).astype(BF16)
        db = do[mine, :]
        q2 = jnp.concatenate([jnp.where(first, qb, zero), jnp.where(first, zero, qb)], axis=0)
        d2 = jnp.concatenate([jnp.where(first, db, zero), jnp.where(first, zero, db)], axis=0)
        qc = jnp.concatenate([q2, ones], axis=1)
        sn = nt(near_k[seen, :], qc)
        sf = nt(far_k[...], qc)
        sn = jnp.concatenate(
            [
                jnp.where(below, sn[:ROWS], DEAD),
                sn[ROWS:WIN],
                jnp.where(above, sn[WIN:], DEAD),
            ],
            axis=0,
        )
        top = jnp.maximum(jnp.max(sn, axis=0, keepdims=True), jnp.max(sf, axis=0, keepdims=True))
        en = jnp.exp(sn - top)
        ef = jnp.exp(sf - top)
        total = jnp.sum(en, axis=0, keepdims=True) + jnp.sum(ef, axis=0, keepdims=True)
        share = 1.0 / total
        wn, wf = en * share, ef * share
        rn, rf = wn.astype(BF16), wf.astype(BF16)
        att = merged(nn(near_vt[:, seen], rn) + nn(far_vt[...], rf))
        out[mine, :] = att.T.astype(out.dtype)
        parts = att * dot[:, mine]
        row_dot = jnp.concatenate(
            [
                jnp.sum(parts[:half], axis=0, keepdims=True),
                jnp.sum(parts[half:], axis=0, keepdims=True),
            ],
            axis=1,
        )
        gn = (wn * (nt(near_v[seen, :], d2) - row_dot)).astype(BF16)
        gf = (wf * (nt(far_v[...], d2) - row_dot)).astype(BF16)
        dqt = merged(nn(near_kt[:, seen], gn) + nn(far_kt[...], gf)) * scale
        dq[mine, :] = dqt.T.astype(dq.dtype)
        near_dk[seen, :] += nn(gn, q2)
        near_dv[seen, :] += nn(rn, d2)
        if b == 0:
            far_dk[...] = nn(gf, q2)
            far_dv[...] = nn(rf, d2)
        else:
            far_dk[...] += nn(gf, q2)
            far_dv[...] += nn(rf, d2)


def tn(a, b):
    return lax.dot_general(a, b, (((0,), (0,)), ((), ())), preferred_element_type=F32)


def kernel(levels, scale, starts, ids, table, q, k, v, do, out, dq, dk, dv, bias, padded,
           send_f, recv_f, send_bias, recv_bias, send_b, recv_b, own,
           near_k, near_v, far_k, far_v, near_kt, near_vt, far_kt, far_vt, dot,
           near_dk, near_dv, far_dk, far_dv,
           sem_fs, sem_fr, sem_bias_s, sem_bias_r, sem_bs, sem_br):
    rows, width_all = q.shape
    pairs = width_all // LANES
    ahead = min(AHEAD, pairs)
    types, heads = table.shape
    lines = lax.axis_size("seq")
    count = lax.axis_size("grp") * lines
    position = lax.axis_index("grp") * lines + lax.axis_index("seq")
    depth = [BLK + (WIN if e == 0 else 0) for e in range(levels)]
    offset = [sum(depth[:e]) for e in range(levels)]
    spot = [pl.ds(offset[e], depth[e]) for e in range(levels)]

    def device(index):
        return (lax.div(index, lines), lax.rem(index, lines))

    def takes(e):
        return position >= 2**e

    def gives(e):
        return position + 2**e < count

    def copy(src, dst, send, recv, index):
        return pltpu.make_async_remote_copy(
            src_ref=src, dst_ref=dst, send_sem=send, recv_sem=recv,
            device_id=device(index), device_id_type=pl.DeviceIdType.MESH,
        )

    def ahead_copy(p, e):
        return copy(send_f.at[p, spot[e]], recv_f.at[p, spot[e]], sem_fs.at[p, e],
                    sem_fr.at[p, e], position + 2**e)

    def bias_copy(e):
        return copy(send_bias.at[spot[e]], recv_bias.at[spot[e]], sem_bias_s.at[e],
                    sem_bias_r.at[e], position + 2**e)

    def back_copy(p, e):
        return copy(send_b.at[p, spot[e]], recv_b.at[p, spot[e]], sem_bs.at[p, e],
                    sem_br.at[p, e], position - 2**e)

    barrier = pltpu.get_barrier_semaphore()
    for e in range(levels):

        @pl.when(gives(e))
        def _():
            pl.semaphore_signal(barrier, inc=1, device_id=device(position + 2**e),
                                device_id_type=pl.DeviceIdType.MESH)

        @pl.when(takes(e))
        def _():
            pl.semaphore_signal(barrier, inc=1, device_id=device(position - 2**e),
                                device_id_type=pl.DeviceIdType.MESH)

    def columns(p):
        return pl.ds(pl.multiple_of(p * LANES, LANES), LANES)

    def gather(p):
        both = jnp.concatenate([k[:, columns(p)], v[:, columns(p)]], axis=1)
        for e in range(levels):
            pick = block_rows_of(starts[0, e], rows)
            send_f[p, offset[e] : offset[e] + BLK, :] = nn(pick, both).astype(BF16)
            if e == 0:
                send_f[p, BLK : BLK + WIN, :] = both[rows - WIN :]

    def send_ahead(p):
        for e in range(levels):

            @pl.when(gives(e))
            def _():
                ahead_copy(p, e).start()

    gather(0)
    greeted = 0
    for e in range(levels):
        greeted = greeted + gives(e).astype(jnp.int32) + takes(e).astype(jnp.int32)
    pl.semaphore_wait(barrier, greeted)
    send_ahead(0)
    padded[...] = jnp.zeros_like(padded)
    padded[:, :heads] = table[...].astype(BF16).astype(F32)
    kind = lax.broadcasted_iota(jnp.int32, (types, rows), 0)
    onehot = (kind == ids[...]).astype(F32).astype(BF16)
    bias[...] = tn(onehot, padded[...].astype(BF16)).astype(BF16)
    for e in range(levels):
        pick = block_rows_of(starts[0, e], rows)
        send_bias[offset[e] : offset[e] + BLK, :] = nn(pick, bias[...]).astype(BF16)
        if e == 0:
            send_bias[BLK : BLK + WIN, :] = bias[rows - WIN :, :]

        @pl.when(jnp.logical_not(takes(e)))
        def _():
            recv_bias[spot[e], :] = jnp.full((depth[e], LANES), DEAD, BF16)

            def clear(p, carry):
                recv_f[p, spot[e], :] = jnp.zeros((depth[e], 2 * LANES), BF16)
                return carry

            lax.fori_loop(0, pairs, clear, 0)

        @pl.when(jnp.logical_not(gives(e)))
        def _():
            def clear(p, carry):
                recv_b[p, spot[e], :] = jnp.zeros((depth[e], 2 * LANES), BF16)
                return carry

            lax.fori_loop(0, pairs, clear, 0)

    for e in range(levels):

        @pl.when(gives(e))
        def _():
            bias_copy(e).start()

    def early(p, carry):
        gather(p)
        send_ahead(p)
        return carry

    lax.fori_loop(1, ahead, early, 0)
    for e in range(levels):

        @pl.when(takes(e))
        def _():
            bias_copy(e).wait_recv()

    near_k[:WIN, LANES:] = recv_bias[BLK : BLK + WIN, :]
    near_k[WIN:, LANES:] = bias[...]
    for e in range(levels):
        far_k[e * BLK : (e + 1) * BLK, LANES:] = recv_bias[offset[e] : offset[e] + BLK, :]

    def one_pair(p, carry):
        mine = columns(p)
        near_k[WIN:, :LANES] = k[:, mine]
        near_v[WIN:, :] = v[:, mine]
        dot[...] = do[:, mine].astype(F32).T
        for e in range(levels):

            @pl.when(takes(e))
            def _():
                ahead_copy(p, e).wait_recv()

        @pl.when(p + ahead < pairs)
        def _():
            gather(p + ahead)
            send_ahead(p + ahead)

        for e in range(levels):
            at = slice(e * BLK, (e + 1) * BLK)
            far_k[at, :LANES] = recv_f[p, offset[e] : offset[e] + BLK, :LANES]
            far_v[at, :] = recv_f[p, offset[e] : offset[e] + BLK, LANES:]
        near_k[:WIN, :LANES] = recv_f[p, BLK : BLK + WIN, :LANES]
        near_v[:WIN, :] = recv_f[p, BLK : BLK + WIN, LANES:]
        near_kt[...] = near_k[:, :LANES].T
        near_vt[...] = near_v[...].T
        far_kt[...] = far_k[:, :LANES].T
        far_vt[...] = far_v[...].T
        attend_pair(2 * p, scale, q.at[:, mine], do.at[:, mine], near_k, near_v, far_k, far_v,
                    near_kt, near_vt, far_kt, far_vt, dot, out.at[:, mine], dq.at[:, mine],
                    near_dk, near_dv, far_dk, far_dv)
        for e in range(levels):
            at = slice(e * BLK, (e + 1) * BLK)
            send_b[p, offset[e] : offset[e] + BLK, :LANES] = far_dk[at, :].astype(BF16)
            send_b[p, offset[e] : offset[e] + BLK, LANES:] = far_dv[at, :].astype(BF16)
            if e == 0:
                send_b[p, BLK : BLK + WIN, :LANES] = near_dk[:WIN, :].astype(BF16)
                send_b[p, BLK : BLK + WIN, LANES:] = near_dv[:WIN, :].astype(BF16)

            @pl.when(takes(e))
            def _():
                back_copy(p, e).start()

        own[p, :, :LANES] = near_dk[WIN:, :]
        own[p, :, LANES:] = near_dv[WIN:, :]
        return carry

    lax.fori_loop(0, pairs, one_pair, 0)

    def settle(p, carry):
        for e in range(levels):

            @pl.when(gives(e))
            def _():
                back_copy(p, e).wait_recv()

        total = own[p]
        for e in range(levels):
            total = total + tn(
                block_rows_of(starts[0, e], rows), recv_b[p, offset[e] : offset[e] + BLK, :]
            )
        first = rows - WIN
        last = total[first:] + recv_b[p, BLK : BLK + WIN, :].astype(F32)
        mine = columns(p)
        dk[:first, mine] = total[:first, :LANES].astype(BF16)
        dv[:first, mine] = total[:first, LANES:].astype(BF16)
        dk[first:, mine] = last[:, :LANES].astype(BF16)
        dv[first:, mine] = last[:, LANES:].astype(BF16)
        return carry

    lax.fori_loop(0, pairs, settle, 0)

    def sent(p, carry):
        for e in range(levels):

            @pl.when(gives(e))
            def _():
                ahead_copy(p, e).wait_send()

            @pl.when(takes(e))
            def _():
                back_copy(p, e).wait_send()

        return carry

    lax.fori_loop(0, pairs, sent, 0)
    for e in range(levels):

        @pl.when(gives(e))
        def _():
            bias_copy(e).wait_send()


def hand_over(*refs):
    for source, target in zip(refs[:4], refs[4:]):
        target[...] = source[...]


def local(queries, keys, values, event_ids, type_bias, block_start, d_out):
    rows, width_all = queries.shape
    types, heads = type_bias.shape
    levels = block_start.shape[1]
    scale = (width_all // heads) ** -0.5
    pairs = width_all // LANES
    far = levels * BLK
    sent = far + WIN
    smem = pl.BlockSpec(memory_space=pltpu.SMEM)
    vmem = pl.BlockSpec(memory_space=pltpu.VMEM)
    dma = pltpu.SemaphoreType.DMA
    held = pl.pallas_call(
        functools.partial(kernel, levels, scale),
        out_shape=[jax.ShapeDtypeStruct((rows, width_all), BF16)] * 4,
        in_specs=[smem] + [vmem] * 6,
        out_specs=[vmem] * 4,
        scratch_shapes=[
            pltpu.VMEM((rows, LANES), BF16),
            pltpu.VMEM((types, LANES), F32),
            pltpu.VMEM((pairs, sent, 2 * LANES), BF16),
            pltpu.VMEM((pairs, sent, 2 * LANES), BF16),
            pltpu.VMEM((sent, LANES), BF16),
            pltpu.VMEM((sent, LANES), BF16),
            pltpu.VMEM((pairs, sent, 2 * LANES), BF16),
            pltpu.VMEM((pairs, sent, 2 * LANES), BF16),
            pltpu.VMEM((pairs, rows, 2 * LANES), F32),
            pltpu.VMEM((WIN + rows, 2 * LANES), BF16),
            pltpu.VMEM((WIN + rows, LANES), BF16),
            pltpu.VMEM((far, 2 * LANES), BF16),
            pltpu.VMEM((far, LANES), BF16),
            pltpu.VMEM((LANES, WIN + rows), BF16),
            pltpu.VMEM((LANES, WIN + rows), BF16),
            pltpu.VMEM((LANES, far), BF16),
            pltpu.VMEM((LANES, far), BF16),
            pltpu.VMEM((LANES, rows), F32),
            pltpu.VMEM((WIN + rows, LANES), F32),
            pltpu.VMEM((WIN + rows, LANES), F32),
            pltpu.VMEM((far, LANES), F32),
            pltpu.VMEM((far, LANES), F32),
            dma((pairs, levels)),
            dma((pairs, levels)),
            dma((levels,)),
            dma((levels,)),
            dma((pairs, levels)),
            dma((pairs, levels)),
        ],
        compiler_params=pltpu.CompilerParams(
            vmem_limit_bytes=56 * 2**20, collective_id=0, has_side_effects=True
        ),
        cost_estimate=pl.CostEstimate(
            flops=12 * rows * (WIN + ROWS + far) * width_all,
            bytes_accessed=16 * rows * width_all,
            transcendentals=rows * (WIN + ROWS + far) * heads,
        ),
        name="attend",
    )(block_start, event_ids[None, :], type_bias, queries, keys, values, d_out)
    part = pl.BlockSpec((ROWS, width_all), lambda i: (i, 0))
    return pl.pallas_call(
        hand_over,
        grid=(rows // ROWS,),
        out_shape=[jax.ShapeDtypeStruct((rows, width_all), BF16)] * 4,
        in_specs=[part] * 4,
        out_specs=[part] * 4,
        name="hand_over",
    )(*held)


def solution(mesh):
    rows = P(AXES, None)
    return jax.shard_map(
        local,
        mesh=mesh,
        in_specs=(rows, rows, rows, P(AXES), P(), rows, rows),
        out_specs=(rows, rows, rows, rows),
        check_vma=False,
    )
```

```python
import functools

import jax
import jax.numpy as jnp
from jax import lax
from jax.experimental import pallas as pl
from jax.experimental.pallas import tpu as pltpu
from jax.sharding import PartitionSpec as P

WIN = 256
BLK = 64
ROWS = 128
LANES = 128
DEAD = -1e30
AHEAD = 1
AXES = ("grp", "seq")
F32 = jnp.float32
BF16 = jnp.bfloat16


def nt(a, b):
    return lax.dot_general(a, b, (((1,), (1,)), ((), ())), preferred_element_type=F32)


def nn(a, b):
    return lax.dot_general(a, b, (((1,), (0,)), ((), ())), preferred_element_type=F32)


def block_rows_of(start, rows):
    t = lax.broadcasted_iota(jnp.int32, (BLK, rows), 0)
    j = lax.broadcasted_iota(jnp.int32, (BLK, rows), 1)
    return (j - t == start).astype(F32).astype(BF16)


def merged(pair):
    half = LANES // 2
    return jnp.concatenate([pair[:half, :ROWS], pair[half:, ROWS:]], axis=0)


def attend_pair(head, scale, q, do, near_k, near_v, far_k, far_v, near_kt, near_vt, far_kt, far_vt,
                dot, out, dq, near_dk, near_dv, far_dk, far_dv):
    rows = q.shape[0]
    half = LANES // 2
    lane = lax.broadcasted_iota(jnp.int32, (ROWS, LANES), 1)
    first = lane < half
    ones = jnp.concatenate([(lane == head).astype(F32), (lane == head + 1).astype(F32)], axis=0)
    ones = ones.astype(BF16)
    span_row = lax.broadcasted_iota(jnp.int32, (ROWS, 2 * ROWS), 0)
    query_col = lax.broadcasted_iota(jnp.int32, (ROWS, 2 * ROWS), 1) & (ROWS - 1)
    below, above = span_row >= query_col, span_row <= query_col
    span = WIN + ROWS
    zero = jnp.zeros((ROWS, LANES), BF16)
    near_dk[...] = jnp.zeros_like(near_dk)
    near_dv[...] = jnp.zeros_like(near_dv)
    for b in range(rows // ROWS):
        mine = slice(b * ROWS, (b + 1) * ROWS)
        seen = slice(b * ROWS, b * ROWS + span)
        qb = (q[mine, :].astype(F32) * scale).astype(BF16)
        db = do[mine, :]
        q2 = jnp.concatenate([jnp.where(first, qb, zero), jnp.where(first, zero, qb)], axis=0)
        d2 = jnp.concatenate([jnp.where(first, db, zero), jnp.where(first, zero, db)], axis=0)
        qc = jnp.concatenate([q2, ones], axis=1)
        sn = nt(near_k[seen, :], qc)
        sf = nt(far_k[...], qc)
        sn = jnp.concatenate(
            [
                jnp.where(below, sn[:ROWS], DEAD),
                sn[ROWS:WIN],
                jnp.where(above, sn[WIN:], DEAD),
            ],
            axis=0,
        )
        top = jnp.maximum(jnp.max(sn, axis=0, keepdims=True), jnp.max(sf, axis=0, keepdims=True))
        en = jnp.exp(sn - top)
        ef = jnp.exp(sf - top)
        total = jnp.sum(en, axis=0, keepdims=True) + jnp.sum(ef, axis=0, keepdims=True)
        share = 1.0 / total
        wn, wf = en * share, ef * share
        rn, rf = wn.astype(BF16), wf.astype(BF16)
        att = merged(nn(near_vt[:, seen], rn) + nn(far_vt[...], rf))
        out[mine, :] = att.T.astype(out.dtype)
        parts = att * dot[:, mine]
        row_dot = jnp.concatenate(
            [
                jnp.sum(parts[:half], axis=0, keepdims=True),
                jnp.sum(parts[half:], axis=0, keepdims=True),
            ],
            axis=1,
        )
        gn = (wn * (nt(near_v[seen, :], d2) - row_dot)).astype(BF16)
        gf = (wf * (nt(far_v[...], d2) - row_dot)).astype(BF16)
        dqt = merged(nn(near_kt[:, seen], gn) + nn(far_kt[...], gf)) * scale
        dq[mine, :] = dqt.T.astype(dq.dtype)
        near_dk[seen, :] += nn(gn, q2)
        near_dv[seen, :] += nn(rn, d2)
        if b == 0:
            far_dk[...] = nn(gf, q2)
            far_dv[...] = nn(rf, d2)
        else:
            far_dk[...] += nn(gf, q2)
            far_dv[...] += nn(rf, d2)


def tn(a, b):
    return lax.dot_general(a, b, (((0,), (0,)), ((), ())), preferred_element_type=F32)


def kernel(levels, scale, starts, ids, table, q, k, v, do, out, dq, dk, dv, bias, padded,
           send_f, recv_f, send_bias, recv_bias, send_b, recv_b, own,
           near_k, near_v, far_k, far_v, near_kt, near_vt, far_kt, far_vt, dot,
           near_dk, near_dv, far_dk, far_dv,
           sem_fs, sem_fr, sem_bias_s, sem_bias_r, sem_bs, sem_br):
    rows, width_all = q.shape
    pairs = width_all // LANES
    ahead = min(AHEAD, pairs)
    types, heads = table.shape
    lines = lax.axis_size("seq")
    count = lax.axis_size("grp") * lines
    position = lax.axis_index("grp") * lines + lax.axis_index("seq")
    depth = [BLK + (WIN if e == 0 else 0) for e in range(levels)]
    offset = [sum(depth[:e]) for e in range(levels)]
    spot = [pl.ds(offset[e], depth[e]) for e in range(levels)]

    def device(index):
        return (lax.div(index, lines), lax.rem(index, lines))

    def takes(e):
        return position >= 2**e

    def gives(e):
        return position + 2**e < count

    def copy(src, dst, send, recv, index):
        return pltpu.make_async_remote_copy(
            src_ref=src, dst_ref=dst, send_sem=send, recv_sem=recv,
            device_id=device(index), device_id_type=pl.DeviceIdType.MESH,
        )

    def ahead_copy(p, e):
        return copy(send_f.at[p, spot[e]], recv_f.at[p, spot[e]], sem_fs.at[p, e],
                    sem_fr.at[p, e], position + 2**e)

    def bias_copy(e):
        return copy(send_bias.at[spot[e]], recv_bias.at[spot[e]], sem_bias_s.at[e],
                    sem_bias_r.at[e], position + 2**e)

    def back_copy(p, e):
        return copy(send_b.at[p, spot[e]], recv_b.at[p, spot[e]], sem_bs.at[p, e],
                    sem_br.at[p, e], position - 2**e)

    barrier = pltpu.get_barrier_semaphore()
    for e in range(levels):

        @pl.when(gives(e))
        def _():
            pl.semaphore_signal(barrier, inc=1, device_id=device(position + 2**e),
                                device_id_type=pl.DeviceIdType.MESH)

        @pl.when(takes(e))
        def _():
            pl.semaphore_signal(barrier, inc=1, device_id=device(position - 2**e),
                                device_id_type=pl.DeviceIdType.MESH)

    def columns(p):
        return pl.ds(pl.multiple_of(p * LANES, LANES), LANES)

    def gather(p):
        both = jnp.concatenate([k[:, columns(p)], v[:, columns(p)]], axis=1)
        for e in range(levels):
            pick = block_rows_of(starts[0, e], rows)
            send_f[p, offset[e] : offset[e] + BLK, :] = nn(pick, both).astype(BF16)
            if e == 0:
                send_f[p, BLK : BLK + WIN, :] = both[rows - WIN :]

    def send_ahead(p):
        for e in range(levels):

            @pl.when(gives(e))
            def _():
                ahead_copy(p, e).start()

    gather(0)
    greeted = 0
    for e in range(levels):
        greeted = greeted + gives(e).astype(jnp.int32) + takes(e).astype(jnp.int32)
    pl.semaphore_wait(barrier, greeted)
    send_ahead(0)
    padded[...] = jnp.zeros_like(padded)
    padded[:, :heads] = table[...].astype(BF16).astype(F32)
    kind = lax.broadcasted_iota(jnp.int32, (types, rows), 0)
    onehot = (kind == ids[...]).astype(F32).astype(BF16)
    bias[...] = tn(onehot, padded[...].astype(BF16)).astype(BF16)
    for e in range(levels):
        pick = block_rows_of(starts[0, e], rows)
        send_bias[offset[e] : offset[e] + BLK, :] = nn(pick, bias[...]).astype(BF16)
        if e == 0:
            send_bias[BLK : BLK + WIN, :] = bias[rows - WIN :, :]

        @pl.when(jnp.logical_not(takes(e)))
        def _():
            recv_bias[spot[e], :] = jnp.full((depth[e], LANES), DEAD, BF16)

            def clear(p, carry):
                recv_f[p, spot[e], :] = jnp.zeros((depth[e], 2 * LANES), BF16)
                return carry

            lax.fori_loop(0, pairs, clear, 0)

        @pl.when(jnp.logical_not(gives(e)))
        def _():
            def clear(p, carry):
                recv_b[p, spot[e], :] = jnp.zeros((depth[e], 2 * LANES), BF16)
                return carry

            lax.fori_loop(0, pairs, clear, 0)

    for e in range(levels):

        @pl.when(gives(e))
        def _():
            bias_copy(e).start()

    def early(p, carry):
        gather(p)
        send_ahead(p)
        return carry

    lax.fori_loop(1, ahead, early, 0)
    for e in range(levels):

        @pl.when(takes(e))
        def _():
            bias_copy(e).wait_recv()

    near_k[:WIN, LANES:] = recv_bias[BLK : BLK + WIN, :]
    near_k[WIN:, LANES:] = bias[...]
    for e in range(levels):
        far_k[e * BLK : (e + 1) * BLK, LANES:] = recv_bias[offset[e] : offset[e] + BLK, :]

    def one_pair(p, carry):
        @pl.when(p + ahead < pairs)
        def _():
            gather(p + ahead)

        mine = columns(p)
        near_k[WIN:, :LANES] = k[:, mine]
        near_v[WIN:, :] = v[:, mine]
        dot[...] = do[:, mine].astype(F32).T
        for e in range(levels):

            @pl.when(takes(e))
            def _():
                ahead_copy(p, e).wait_recv()

        @pl.when(p + ahead < pairs)
        def _():
            send_ahead(p + ahead)

        for e in range(levels):
            at = slice(e * BLK, (e + 1) * BLK)
            far_k[at, :LANES] = recv_f[p, offset[e] : offset[e] + BLK, :LANES]
            far_v[at, :] = recv_f[p, offset[e] : offset[e] + BLK, LANES:]
        near_k[:WIN, :LANES] = recv_f[p, BLK : BLK + WIN, :LANES]
        near_v[:WIN, :] = recv_f[p, BLK : BLK + WIN, LANES:]
        near_kt[...] = near_k[:, :LANES].T
        near_vt[...] = near_v[...].T
        far_kt[...] = far_k[:, :LANES].T
        far_vt[...] = far_v[...].T
        attend_pair(2 * p, scale, q.at[:, mine], do.at[:, mine], near_k, near_v, far_k, far_v,
                    near_kt, near_vt, far_kt, far_vt, dot, out.at[:, mine], dq.at[:, mine],
                    near_dk, near_dv, far_dk, far_dv)
        for e in range(levels):
            at = slice(e * BLK, (e + 1) * BLK)
            send_b[p, offset[e] : offset[e] + BLK, :LANES] = far_dk[at, :].astype(BF16)
            send_b[p, offset[e] : offset[e] + BLK, LANES:] = far_dv[at, :].astype(BF16)
            if e == 0:
                send_b[p, BLK : BLK + WIN, :LANES] = near_dk[:WIN, :].astype(BF16)
                send_b[p, BLK : BLK + WIN, LANES:] = near_dv[:WIN, :].astype(BF16)

            @pl.when(takes(e))
            def _():
                back_copy(p, e).start()

        own[p, :, :LANES] = near_dk[WIN:, :]
        own[p, :, LANES:] = near_dv[WIN:, :]
        return carry

    lax.fori_loop(0, pairs, one_pair, 0)

    def settle(p, carry):
        for e in range(levels):

            @pl.when(gives(e))
            def _():
                back_copy(p, e).wait_recv()

        total = own[p]
        for e in range(levels):
            total = total + tn(
                block_rows_of(starts[0, e], rows), recv_b[p, offset[e] : offset[e] + BLK, :]
            )
        first = rows - WIN
        last = total[first:] + recv_b[p, BLK : BLK + WIN, :].astype(F32)
        mine = columns(p)
        dk[:first, mine] = total[:first, :LANES].astype(BF16)
        dv[:first, mine] = total[:first, LANES:].astype(BF16)
        dk[first:, mine] = last[:, :LANES].astype(BF16)
        dv[first:, mine] = last[:, LANES:].astype(BF16)
        return carry

    lax.fori_loop(0, pairs, settle, 0)

    def sent(p, carry):
        for e in range(levels):

            @pl.when(gives(e))
            def _():
                ahead_copy(p, e).wait_send()

            @pl.when(takes(e))
            def _():
                back_copy(p, e).wait_send()

        return carry

    lax.fori_loop(0, pairs, sent, 0)
    for e in range(levels):

        @pl.when(gives(e))
        def _():
            bias_copy(e).wait_send()


def hand_over(*refs):
    for source, target in zip(refs[:4], refs[4:]):
        target[...] = source[...]


def local(queries, keys, values, event_ids, type_bias, block_start, d_out):
    rows, width_all = queries.shape
    types, heads = type_bias.shape
    levels = block_start.shape[1]
    scale = (width_all // heads) ** -0.5
    pairs = width_all // LANES
    far = levels * BLK
    sent = far + WIN
    smem = pl.BlockSpec(memory_space=pltpu.SMEM)
    vmem = pl.BlockSpec(memory_space=pltpu.VMEM)
    dma = pltpu.SemaphoreType.DMA
    held = pl.pallas_call(
        functools.partial(kernel, levels, scale),
        out_shape=[jax.ShapeDtypeStruct((rows, width_all), BF16)] * 4,
        in_specs=[smem] + [vmem] * 6,
        out_specs=[vmem] * 4,
        scratch_shapes=[
            pltpu.VMEM((rows, LANES), BF16),
            pltpu.VMEM((types, LANES), F32),
            pltpu.VMEM((pairs, sent, 2 * LANES), BF16),
            pltpu.VMEM((pairs, sent, 2 * LANES), BF16),
            pltpu.VMEM((sent, LANES), BF16),
            pltpu.VMEM((sent, LANES), BF16),
            pltpu.VMEM((pairs, sent, 2 * LANES), BF16),
            pltpu.VMEM((pairs, sent, 2 * LANES), BF16),
            pltpu.VMEM((pairs, rows, 2 * LANES), F32),
            pltpu.VMEM((WIN + rows, 2 * LANES), BF16),
            pltpu.VMEM((WIN + rows, LANES), BF16),
            pltpu.VMEM((far, 2 * LANES), BF16),
            pltpu.VMEM((far, LANES), BF16),
            pltpu.VMEM((LANES, WIN + rows), BF16),
            pltpu.VMEM((LANES, WIN + rows), BF16),
            pltpu.VMEM((LANES, far), BF16),
            pltpu.VMEM((LANES, far), BF16),
            pltpu.VMEM((LANES, rows), F32),
            pltpu.VMEM((WIN + rows, LANES), F32),
            pltpu.VMEM((WIN + rows, LANES), F32),
            pltpu.VMEM((far, LANES), F32),
            pltpu.VMEM((far, LANES), F32),
            dma((pairs, levels)),
            dma((pairs, levels)),
            dma((levels,)),
            dma((levels,)),
            dma((pairs, levels)),
            dma((pairs, levels)),
        ],
        compiler_params=pltpu.CompilerParams(
            vmem_limit_bytes=56 * 2**20, collective_id=0, has_side_effects=True
        ),
        cost_estimate=pl.CostEstimate(
            flops=12 * rows * (WIN + ROWS + far) * width_all,
            bytes_accessed=16 * rows * width_all,
            transcendentals=rows * (WIN + ROWS + far) * heads,
        ),
        name="attend",
    )(block_start, event_ids[None, :], type_bias, queries, keys, values, d_out)
    part = pl.BlockSpec((ROWS, width_all), lambda i: (i, 0))
    return pl.pallas_call(
        hand_over,
        grid=(rows // ROWS,),
        out_shape=[jax.ShapeDtypeStruct((rows, width_all), BF16)] * 4,
        in_specs=[part] * 4,
        out_specs=[part] * 4,
        name="hand_over",
    )(*held)


def solution(mesh):
    rows = P(AXES, None)
    return jax.shard_map(
        local,
        mesh=mesh,
        in_specs=(rows, rows, rows, P(AXES), P(), rows, rows),
        out_specs=(rows, rows, rows, rows),
        check_vma=False,
    )
```
